256 devices in a mesh: rcv: 16 (over z_hi, x), tf: 16 (over y, z_lo, core).
Axes of the slice: x: 4, y: 4, z: 8 (z_hi: 4, z_lo: 2; z = z_hi * 2 + z_lo), core: 2. Of those that a mesh axis runs over, the one named last changes fastest.
Arguments:
- observed: bfloat16 [2, 16384, 4096], P(None, 'rcv', 'tf'), may hold values from -200 to 200
- synthetic: bfloat16 [2, 16384, 4096], P(None, 'rcv', 'tf'), may hold values from -100 to 100
- live: int32 [2, 16384], P(None, 'rcv'), may hold values 0 or 1
- bins: int32 [1024], replicated, may hold values from 1 to 2047
Outputs:
- adjoint: bfloat16 [2, 16384, 4096], P(None, 'rcv', 'tf')
The draws below stay inside these ranges and needn't reach their ends.
All inputs are finite; a program needn't handle non-finite values. No bound on the sum of `live` on one device may be relied on, other than what follows from the above.
Results may differ from the reference program's by a relative error of at most 0.0041.
The reference program's roundings to bfloat16 on the way count: a program that leaves them out, or rounds other values in their place, can miss the bound.
Values may be sent and summed in bfloat16 or wider, within the bound.
A program may use at most 128 MiB of HBM per device.

```python
import math
import jax
import jax.numpy as jnp

NT = 4096
NF = 1024
S = 2
R = 16384


def band_bins(key):
    key = jax.random.fold_in(key, 101)
    key_vals, key_perm = jax.random.split(key)
    inner = jax.random.randint(key_vals, (NF - 2,), 1, NT // 2).astype(jnp.int32)
    ends = jnp.array([1, NT // 2 - 1], dtype=jnp.int32)
    joined = jnp.concatenate([ends, inner])
    order = jax.random.permutation(key_perm, NF)
    return joined[order]


def signal_pair(key, spread):
    bins = band_bins(key)
    keys = jax.random.split(key, 9)
    tone_count = 8
    floor = (NT / 21400.0) ** 0.5
    base = jnp.clip(jax.random.normal(keys[0], (S, R, NT), jnp.float32), -5.0, 5.0)
    noise = jnp.clip(jax.random.normal(keys[1], (S, R, NT), jnp.float32), -5.0, 5.0)
    where = jnp.arange(R, dtype=jnp.float32) / R
    amp = 0.6 * spread ** where * jax.random.uniform(keys[2], (R,), jnp.float32, 0.7, 1.3)
    gain = jax.random.uniform(keys[3], (S, R), jnp.float32, 0.5, 2.0)
    common = jax.random.randint(keys[4], (S,), 0, 8).astype(jnp.int32)
    jitter = (jax.random.randint(keys[5], (S, R), 0, 4) == 0).astype(jnp.int32)
    shift = common[:, None] + jitter
    stride = NF // (S * tone_count)
    slots = (jnp.arange(S, dtype=jnp.int32)[:, None] * tone_count + jnp.arange(tone_count, dtype=jnp.int32)[None, :]) * stride
    freq = bins[slots]
    level = jax.random.uniform(keys[6], (S, tone_count), jnp.float32, 0.3, 1.5)
    phase = jax.random.uniform(keys[7], (S, R, tone_count), jnp.float32, -math.pi, math.pi)
    factor = jax.random.uniform(keys[8], (S, R, tone_count), jnp.float32, 0.5, 1.5)
    times = jnp.arange(NT, dtype=jnp.int32)
    tone = jnp.zeros((S, R, NT), jnp.float32)
    for index in range(tone_count):
        turns = (times[None, None, :] * freq[:, index][:, None, None] % NT).astype(jnp.float32)
        angle = turns * (2.0 * math.pi / NT) + phase[:, :, index][:, :, None]
        tone = tone + level[:, index][:, None, None] * factor[:, :, index][:, :, None] * jnp.cos(angle)
    signal = floor * base + 0.5 * tone
    position = (times[None, None, :] - shift[:, :, None]) % NT
    moved = jnp.take_along_axis(signal, position, axis=2)
    synth = amp[None, :, None] * signal
    record = amp[None, :, None] * (gain[:, :, None] * moved + 0.7 * floor * noise)
    return (record, synth)


def draw_observed(key, part):
    spread = 3.0
    return signal_pair(key, spread)[0].astype(jnp.bfloat16)


def draw_synthetic(key, part):
    spread = 3.0
    return signal_pair(key, spread)[1].astype(jnp.bfloat16)


def draw_bins(key, part):
    return band_bins(key)


def touch_ends(values, rng, smallest, top_value):
    dims = values.shape
    place = [jax.random.randint(jax.random.fold_in(rng, axis), (), 0, dims[axis]) for axis in range(len(dims))]
    values = values.at[tuple(place)].set(smallest)
    longest = dims.index(max(dims))
    place[longest] = (place[longest] + 1) % dims[longest]
    return values.at[tuple(place)].set(top_value)


def setup_inputs(seed: int = 0) -> dict:
    splits = jax.random.split(jax.random.key(seed), 5)
    observed = draw_observed(jax.random.fold_in(splits[4], 71), 0)
    synthetic = draw_synthetic(jax.random.fold_in(splits[4], 71), 0)
    live = touch_ends((jax.random.randint(splits[2], (S, R), 0, 4) < 3).astype(jnp.int32), jax.random.fold_in(splits[2], 1), 0, 1)
    bins = draw_bins(jax.random.fold_in(splits[4], 71), 0)
    return dict(observed=observed, synthetic=synthetic, live=live, bins=bins)


def tables(bins):
    times = jnp.arange(NT, dtype=jnp.int32)
    angle = ((times[:, None] * bins[None, :]) % NT).astype(jnp.float32) * (2.0 * math.pi / NT)
    scale = NT ** -0.5
    return (jnp.cos(angle) * scale).astype(jnp.bfloat16), (-jnp.sin(angle) * scale).astype(jnp.bfloat16)


def reference(observed, synthetic, live, bins):
    cos_tab, sin_tab = tables(bins)
    outputs = []
    for shot in range(S):
        obs_re = jnp.dot(observed[shot], cos_tab, preferred_element_type=jnp.float32)
        obs_im = jnp.dot(observed[shot], sin_tab, preferred_element_type=jnp.float32)
        syn_re = jnp.dot(synthetic[shot], cos_tab, preferred_element_type=jnp.float32)
        syn_im = jnp.dot(synthetic[shot], sin_tab, preferred_element_type=jnp.float32)
        weight = live[shot].astype(jnp.float32)[:, None]
        cross_re = jnp.sum(weight * (syn_re * obs_re + syn_im * obs_im), axis=0)
        cross_im = jnp.sum(weight * (syn_re * obs_im - syn_im * obs_re), axis=0)
        power = jnp.sum(weight * (syn_re * syn_re + syn_im * syn_im), axis=0)
        denom = power + 0.001 * jnp.max(power)
        w_re = cross_re / denom
        w_im = cross_im / denom
        res_re = (weight * (w_re * syn_re - w_im * syn_im - obs_re)).astype(jnp.bfloat16)
        res_im = (weight * (w_re * syn_im + w_im * syn_re - obs_im)).astype(jnp.bfloat16)
        total = jnp.dot(res_re, cos_tab.T, preferred_element_type=jnp.float32)
        total = total + jnp.dot(res_im, sin_tab.T, preferred_element_type=jnp.float32)
        outputs.append((2.0 * total).astype(jnp.bfloat16))
    return jnp.stack(outputs)
```

```python
import math

import jax
import jax.numpy as jnp
from jax import lax
from jax.experimental import pallas as pl
from jax.experimental.pallas import tpu as pltpu
from jax.sharding import PartitionSpec as P

NT = 4096
MESH = pl.DeviceIdType.MESH
N_TF = 16
N_Y = 4
N_J = 4
SPAN = NT // N_TF
QUART = NT // N_Y
NF = 1024
SEED = 64
SLOTS = ((2, 0), (2, 1), (2, 2), (2, 3), (3, 0), (1, 0), (3, 1), (1, 1),
         (3, 2), (1, 2), (3, 3), (1, 3), (0, 2), (0, 3), (0, 1))


def cos_sin(turns):
    k = turns & (NT - 1)
    quadrant = (k + NT // 8) // (NT // 4)
    angle = (k - quadrant * (NT // 4)).astype(jnp.float32) * (2.0 * math.pi / NT)
    sq = angle * angle
    s = angle + angle * sq * (-1 / 6 + sq * (1 / 120 + sq * (-1 / 5040 + sq * (1 / 362880))))
    c = 1.0 + sq * (-0.5 + sq * (1 / 24 + sq * (-1 / 720 + sq * (1 / 40320))))
    odd = (quadrant & 1) == 1
    cos = jnp.where(odd, s, c)
    sin = jnp.where(odd, c, s)
    turn = quadrant & 3
    cos = jnp.where((turn == 1) | (turn == 2), -cos, cos)
    sin = jnp.where(turn >= 2, -sin, sin)
    return cos, sin


def peer_of(y, j, dy, dj):
    dz, dc = dj // 2, dj % 2
    z = (j // 2 + dz) % 2
    c = (j + dc) % 2
    return (y + dy) % N_Y, z * 2 + c


def wait_bytes(view, sem):
    pltpu.make_async_copy(view, view, sem).wait()


def kernel(r_sub, n_x, n_zh, bins_ref, live_ref, obs_ref, syn_ref, out_ref,
           xbuf, tab, seed, first, rot, spec, res, outbuf, wrow,
           part, from_tf, sum_tf, from_x, sum_x, from_z, total,
           in_send, in_recv, tf_send, tf_recv, x_send, x_recv, z_send, z_recv, out_send, out_recv):
    me = lax.axis_index("tf")
    mr = lax.axis_index("rcv")
    y = me // N_J
    j = me % N_J
    x = mr % n_x
    zh = mr // n_x
    shots = 2
    rows = 2 * r_sub

    barrier = pltpu.get_barrier_semaphore()
    count = 0
    for dx in range(1, n_x):
        pl.semaphore_signal(barrier, inc=1, device_id={"rcv": zh * n_x + (x + dx) % n_x}, device_id_type=MESH)
        count += 1
    for dz in range(1, n_zh):
        pl.semaphore_signal(barrier, inc=1, device_id={"rcv": ((zh + dz) % n_zh) * n_x + x}, device_id_type=MESH)
        count += 1
    for dy, dj in SLOTS:
        py, pj = peer_of(y, j, dy, dj)
        pl.semaphore_signal(barrier, inc=1, device_id={"tf": py * N_J + pj}, device_id_type=MESH)
        count += 1
    pl.semaphore_wait(barrier, count)

    def landing(s, a):
        row = pl.multiple_of(y * rows + a * r_sub, r_sub)
        return xbuf.at[s, pl.ds(row, r_sub), pl.ds(pl.multiple_of(j * SPAN, SPAN), SPAN)]

    for s in range(shots):
        for dy, dj in SLOTS:
            py, pj = peer_of(y, j, dy, dj)
            peer = py * N_J + pj
            for a, ref in enumerate((obs_ref, syn_ref)):
                pltpu.make_async_remote_copy(
                    src_ref=ref.at[s, pl.ds(pl.multiple_of(peer * r_sub, r_sub), r_sub), :],
                    dst_ref=landing(s, a), send_sem=in_send.at[s], recv_sem=in_recv.at[s],
                    device_id={"tf": peer}, device_id_type=MESH).start()
        for a, ref in enumerate((obs_ref, syn_ref)):
            pltpu.make_async_copy(
                ref.at[s, pl.ds(pl.multiple_of(me * r_sub, r_sub), r_sub), :],
                landing(s, a), in_recv.at[s]).start()

    bins = bins_ref[...]
    times = lax.broadcasted_iota(jnp.int32, (SEED, NF), 0)
    cos, sin = cos_sin(times * bins)
    scale = NT ** (-0.5)
    seed[0] = cos * scale
    seed[1] = sin * scale
    steps = QUART // SEED
    times = lax.broadcasted_iota(jnp.int32, (steps, NF), 0) * SEED
    cos, sin = cos_sin(times * bins)
    first[0] = cos
    first[1] = sin
    turn = bins & 3
    rot[0:1, :] = jnp.where(turn == 0, 1.0, jnp.where(turn == 2, -1.0, 0.0))
    rot[1:2, :] = jnp.where(turn == 1, 1.0, jnp.where(turn == 3, -1.0, 0.0))
    rot[2:3, :] = jnp.where((turn & 1) == 0, 1.0, -1.0)

    def make_rows(i, carry):
        c0 = first[0, pl.ds(i, 1), :]
        s0 = first[1, pl.ds(i, 1), :]
        at = pl.ds(pl.multiple_of(i * SEED, SEED), SEED)
        c1 = seed[0]
        s1 = seed[1]
        tab[at, :NF] = (c0 * c1 - s0 * s1).astype(jnp.bfloat16)
        tab[at, NF:] = (-(s0 * c1 + c0 * s1)).astype(jnp.bfloat16)
        return carry

    lax.fori_loop(0, steps, make_rows, 0)

    r_dev = live_ref.shape[1]
    lane = lax.broadcasted_iota(jnp.int32, (r_sub, r_dev), 1)
    line = lax.broadcasted_iota(jnp.int32, (r_sub, r_dev), 0) + me * r_sub
    weights = []
    for s in range(shots):
        flags = jnp.where(lane == line, live_ref[s:s + 1, :].astype(jnp.float32), 0.0)
        weights.append(jnp.sum(flags, axis=1, keepdims=True))

    def forward(s):
        weight = weights[s]
        width = 256

        def tile(n, carry):
            lanes = pl.ds(pl.multiple_of(n * width, width), width)
            lanes_im = pl.ds(pl.multiple_of(NF + n * width, width), width)
            traces = xbuf[s]
            re = jnp.dot(traces, tab[:, lanes], preferred_element_type=jnp.float32)
            im = jnp.dot(traces, tab[:, lanes_im], preferred_element_type=jnp.float32)
            c1 = rot[0:1, lanes]
            s1 = rot[1:2, lanes]
            sg = rot[2:3, lanes]
            re0, re1, re2, re3 = (re[q * rows:(q + 1) * rows] for q in range(N_Y))
            im0, im1, im2, im3 = (im[q * rows:(q + 1) * rows] for q in range(N_Y))
            x_re = re0 + sg * re2 + c1 * (re1 + re3) + s1 * (im1 - im3)
            x_im = im0 + sg * im2 + c1 * (im1 + im3) + s1 * (re3 - re1)
            obs_re = weight * x_re[:r_sub]
            obs_im = weight * x_im[:r_sub]
            syn_re = weight * x_re[r_sub:]
            syn_im = weight * x_im[r_sub:]
            spec[0, :, lanes] = obs_re
            spec[1, :, lanes] = obs_im
            spec[2, :, lanes] = syn_re
            spec[3, :, lanes] = syn_im
            sums = (
                jnp.sum(syn_re * obs_re + syn_im * obs_im, axis=0, keepdims=True),
                jnp.sum(syn_re * obs_im - syn_im * obs_re, axis=0, keepdims=True),
                jnp.sum(syn_re * syn_re + syn_im * syn_im, axis=0, keepdims=True),
            )
            for q in range(3):
                for h in range(width // 128):
                    part[s, pl.ds(q * 8 + n * (width // 128) + h, 1), :] = sums[q][:, h * 128:(h + 1) * 128]
            return carry

        lax.fori_loop(0, NF // width, tile, 0)

    def reduce(s):
        for dy, dj in SLOTS:
            py, pj = peer_of(y, j, dy, dj)
            pltpu.make_async_remote_copy(
                src_ref=part.at[s], dst_ref=from_tf.at[s, me], send_sem=tf_send.at[s], recv_sem=tf_recv.at[s],
                device_id={"tf": py * N_J + pj}, device_id_type=MESH).start()
        from_tf[s, pl.ds(me, 1)] = part[s][None]
        wait_bytes(from_tf.at[s, pl.ds(0, N_TF - 1)], tf_recv.at[s])
        sum_tf[s] = jnp.sum(from_tf[s], axis=0)
        src, done = sum_tf, from_tf
        for buf, dst, size, pos, send, recv in (
            (from_x, sum_x, n_x, x, x_send, x_recv),
            (from_z, total, n_zh, zh, z_send, z_recv),
        ):
            for d in range(1, size):
                there = zh * n_x + (x + d) % n_x if buf is from_x else ((zh + d) % n_zh) * n_x + x
                pltpu.make_async_remote_copy(
                    src_ref=src.at[s], dst_ref=buf.at[s, pos], send_sem=send.at[s], recv_sem=recv.at[s],
                    device_id={"rcv": there}, device_id_type=MESH).start()
            buf[s, pl.ds(pos, 1)] = src[s][None]
            if size > 1:
                wait_bytes(buf.at[s, pl.ds(0, size - 1)], recv.at[s])
            dst[s] = jnp.sum(buf[s], axis=0)
            src = dst

    def inverse(s):
        cross_re = total[s, 0:8, :]
        cross_im = total[s, 8:16, :]
        power = total[s, 16:24, :]
        denom = power + 0.001 * jnp.max(power)
        wrow[0:8, :] = cross_re / denom
        wrow[8:16, :] = cross_im / denom

        def block(k, carry):
            lanes = pl.ds(pl.multiple_of(k * 128, 128), 128)
            lanes_im = pl.ds(pl.multiple_of(NF + k * 128, 128), 128)
            w_re = wrow[pl.ds(k, 1), :]
            w_im = wrow[pl.ds(8 + k, 1), :]
            obs_re, obs_im, syn_re, syn_im = (spec[i, :, lanes] for i in range(4))
            re = w_re * syn_re - w_im * syn_im - obs_re
            im = w_re * syn_im + w_im * syn_re - obs_im
            c1 = rot[0:1, lanes]
            s1 = rot[1:2, lanes]
            sg = rot[2:3, lanes]
            turned = (
                (re, im),
                (c1 * re - s1 * im, s1 * re + c1 * im),
                (sg * re, sg * im),
                (c1 * re + s1 * im, c1 * im - s1 * re),
            )
            for q in range(N_Y):
                res[q * r_sub:(q + 1) * r_sub, lanes] = turned[q][0].astype(jnp.bfloat16)
                res[q * r_sub:(q + 1) * r_sub, lanes_im] = turned[q][1].astype(jnp.bfloat16)
            return carry

        lax.fori_loop(0, NF // 128, block, 0)

        for dj in (2, 3, 1, 0):
            _, pj = peer_of(y, j, 0, dj)
            cols = pl.ds(pl.multiple_of(pj * SPAN, SPAN), SPAN)
            sums = lax.dot_general(res[...], tab[cols, :], (((1,), (1,)), ((), ())),
                                   preferred_element_type=jnp.float32)
            outbuf[s, :, cols] = (2.0 * sums).astype(jnp.bfloat16)
            for dy in (2, 3, 1, 0):
                py, _ = peer_of(y, j, dy, 0)
                src = outbuf.at[s, pl.ds(pl.multiple_of(py * r_sub, r_sub), r_sub), cols]
                dst = out_ref.at[s, pl.ds(pl.multiple_of(me * r_sub, r_sub), r_sub), :]
                if dy == 0 and dj == 0:
                    pltpu.make_async_copy(src, dst, out_recv.at[s]).start()
                else:
                    pltpu.make_async_remote_copy(
                        src_ref=src, dst_ref=dst, send_sem=out_send.at[s], recv_sem=out_recv.at[s],
                        device_id={"tf": py * N_J + pj}, device_id_type=MESH).start()

    for s in range(shots):
        wait_bytes(xbuf.at[s], in_recv.at[s])
        forward(s)
        reduce(s)
        inverse(s)

    for s in range(shots):
        wait_bytes(out_ref.at[s], out_recv.at[s])
    for s in range(shots):
        sent = obs_ref.at[s, pl.ds(0, (N_TF - 1) * r_sub), :]
        wait_bytes(sent, in_send.at[s])
        wait_bytes(sent, in_send.at[s])
        wait_bytes(out_ref.at[s, pl.ds(0, (N_TF - 1) * r_sub), :], out_send.at[s])
        wait_bytes(from_tf.at[s, pl.ds(0, N_TF - 1)], tf_send.at[s])
        if n_x > 1:
            wait_bytes(from_x.at[s, pl.ds(0, n_x - 1)], x_send.at[s])
        if n_zh > 1:
            wait_bytes(from_z.at[s, pl.ds(0, n_zh - 1)], z_send.at[s])


def on_device(n_rcv, observed, synthetic, live, bins):
    shots, r_dev, _ = observed.shape
    r_sub = r_dev // N_TF
    n_x = min(4, n_rcv)
    n_zh = n_rcv // n_x

    def body(*refs):
        kernel(r_sub, n_x, n_zh, *refs)

    f32, bf16 = jnp.float32, jnp.bfloat16
    sums = (24, 128)
    dma = pltpu.SemaphoreType.DMA
    return pl.pallas_call(
        body,
        out_shape=jax.ShapeDtypeStruct(observed.shape, bf16),
        in_specs=[pl.BlockSpec(memory_space=pltpu.VMEM)] * 2 + [pl.BlockSpec(memory_space=pl.ANY)] * 2,
        out_specs=pl.BlockSpec(memory_space=pl.ANY),
        scratch_shapes=[
            pltpu.VMEM((shots, N_Y * 2 * r_sub, QUART), bf16),
            pltpu.VMEM((QUART, 2 * NF), bf16),
            pltpu.VMEM((2, SEED, NF), f32),
            pltpu.VMEM((2, QUART // SEED, NF), f32),
            pltpu.VMEM((8, NF), f32),
            pltpu.VMEM((4, r_sub, NF), f32),
            pltpu.VMEM((N_Y * r_sub, 2 * NF), bf16),
            pltpu.VMEM((shots, N_Y * r_sub, QUART), bf16),
            pltpu.VMEM((16, 128), f32),
            pltpu.VMEM((shots,) + sums, f32),
            pltpu.VMEM((shots, N_TF) + sums, f32),
            pltpu.VMEM((shots,) + sums, f32),
            pltpu.VMEM((shots, n_x) + sums, f32),
            pltpu.VMEM((shots,) + sums, f32),
            pltpu.VMEM((shots, n_zh) + sums, f32),
            pltpu.VMEM((shots,) + sums, f32),
        ] + [dma((shots,))] * 10,
        compiler_params=pltpu.CompilerParams(
            collective_id=0, has_side_effects=True, vmem_limit_bytes=48 * 2 ** 20),
    )(bins.reshape(1, NF), live, observed, synthetic)


def solution(mesh):
    n_rcv = mesh.shape["rcv"]

    def run(*args):
        return on_device(n_rcv, *args)

    in_specs = (P(None, "rcv", "tf"), P(None, "rcv", "tf"), P(None, "rcv"), P())
    out_specs = P(None, "rcv", "tf")
    return jax.shard_map(run, mesh=mesh, in_specs=in_specs, out_specs=out_specs, check_vma=False)
```

```python
import math

import jax
import jax.numpy as jnp
from jax import lax
from jax.experimental import pallas as pl
from jax.experimental.pallas import tpu as pltpu
from jax.sharding import PartitionSpec as P

NT = 4096
MESH = pl.DeviceIdType.MESH
N_TF = 16
N_Y = 4
N_J = 4
SPAN = NT // N_TF
QUART = NT // N_Y
NF = 1024
SEED = 64
SLOTS = ((2, 0), (2, 1), (2, 2), (2, 3), (3, 0), (1, 0), (3, 1), (1, 1),
         (3, 2), (1, 2), (3, 3), (1, 3), (0, 2), (0, 3), (0, 1))

BATCH = (4, 15)
ORDER = (2, 3, 1, 0)
GROUPS = ((0, 3), (3, 4))
X_STEPS = (2, 1, 3)
Z_STEPS = ((2, 0), (2, 1), (1, 1), (3, 1), (1, 0), (3, 0), (0, 1))
TILES = (3, 1, 2, 0)
UNROLL = True


def cos_sin(turns):
    k = turns & (NT - 1)
    quadrant = (k + NT // 8) // (NT // 4)
    angle = (k - quadrant * (NT // 4)).astype(jnp.float32) * (2.0 * math.pi / NT)
    sq = angle * angle
    s = angle + angle * sq * (-1 / 6 + sq * (1 / 120 + sq * (-1 / 5040 + sq * (1 / 362880))))
    c = 1.0 + sq * (-0.5 + sq * (1 / 24 + sq * (-1 / 720 + sq * (1 / 40320))))
    odd = (quadrant & 1) == 1
    cos = jnp.where(odd, s, c)
    sin = jnp.where(odd, c, s)
    turn = quadrant & 3
    cos = jnp.where((turn == 1) | (turn == 2), -cos, cos)
    sin = jnp.where(turn >= 2, -sin, sin)
    return cos, sin


def peer_of(y, j, dy, dj):
    dz, dc = dj // 2, dj % 2
    z = (j // 2 + dz) % 2
    c = (j + dc) % 2
    return (y + dy) % N_Y, z * 2 + c


def wait_bytes(view, sem):
    pltpu.make_async_copy(view, view, sem).wait()


def kernel(r_sub, n_x, n_zh, bins_hbm, live_hbm, obs_ref, syn_ref, out_ref,
           bins_ref, live_ref, xbuf, tab, seed, first, rot, spec, res, outbuf, wrow,
           acc, part, from_a, sum_a, from_x, sum_x, from_z, total,
           small, in_send, in_recv, a_send, a_recv, x_send, x_recv, z_send, z_recv, out_send, out_recv):
    me = lax.axis_index("tf")
    mr = lax.axis_index("rcv")
    y = me // N_J
    j = me % N_J
    x = mr % n_x
    zh = mr // n_x
    shots = 2
    rows = 2 * r_sub

    z_lo = j // 2
    core = j % 2
    z = zh * 2 + z_lo
    n_z = 2 * n_zh

    def stage(k):
        return (
            (part, from_a, sum_a, 2 * N_Y, y * 2 + core, a_send, a_recv),
            (sum_a, from_x, sum_x, n_x, x, x_send, x_recv),
            (sum_x, from_z, total, n_z, z, z_send, z_recv),
        )[k]

    def reduce_peers(k):
        if k == 0:
            return [{"tf": ((y + dy) % N_Y) * N_J + z_lo * 2 + (core + dc) % 2}
                    for dy, dc in ((2, 0), (2, 1), (1, 0), (3, 0), (1, 1), (3, 1), (0, 1))]
        if k == 1:
            return [{"rcv": zh * n_x + (x + d) % n_x} for d in X_STEPS if d < n_x]
        return [{"rcv": ((zh + dh) % n_zh) * n_x + x, "tf": y * N_J + ((z_lo + dl) % 2) * 2 + core}
                for dh, dl in Z_STEPS if dh < n_zh]

    flags = (pltpu.make_async_copy(bins_hbm, bins_ref, small.at[0]),
             pltpu.make_async_copy(live_hbm, live_ref, small.at[1]))
    for copy in flags:
        copy.start()

    barrier = pltpu.get_barrier_semaphore()
    count = 0
    greeted = [peer for peer, (dh, _) in zip(reduce_peers(2), Z_STEPS) if dh > 0] + reduce_peers(1)
    for peer in greeted:
        pl.semaphore_signal(barrier, inc=1, device_id=peer, device_id_type=MESH)
        count += 1
    for dy, dj in SLOTS:
        py, pj = peer_of(y, j, dy, dj)
        pl.semaphore_signal(barrier, inc=1, device_id={"tf": py * N_J + pj}, device_id_type=MESH)
        count += 1
    pl.semaphore_wait(barrier, count)

    def landing(s, a, dy):
        row = ORDER.index(dy) * rows + a * r_sub
        return xbuf.at[s, pl.ds(row, r_sub), pl.ds(pl.multiple_of(j * SPAN, SPAN), SPAN)]

    def send_in(s, slots):
        for dy, dj in slots:
            py, pj = peer_of(y, j, dy, dj)
            peer = py * N_J + pj
            for a, ref in enumerate((obs_ref, syn_ref)):
                pltpu.make_async_remote_copy(
                    src_ref=ref.at[s, pl.ds(pl.multiple_of(peer * r_sub, r_sub), r_sub), :],
                    dst_ref=landing(s, a, dy), send_sem=in_send.at[s], recv_sem=in_recv.at[s, ORDER.index(dy)],
                    device_id={"tf": peer}, device_id_type=MESH).start()

    for s in range(shots):
        for a, ref in enumerate((obs_ref, syn_ref)):
            pltpu.make_async_copy(
                ref.at[s, pl.ds(pl.multiple_of(me * r_sub, r_sub), r_sub), :],
                landing(s, a, 0), in_recv.at[s, ORDER.index(0)]).start()
    send_in(0, SLOTS)
    send_in(1, SLOTS[:BATCH[0]])
    for copy in flags:
        copy.wait()

    bins = bins_ref[...]
    times = lax.broadcasted_iota(jnp.int32, (SEED, NF), 0)
    cos, sin = cos_sin(times * bins)
    scale = NT ** (-0.5)
    seed[0] = cos * scale
    seed[1] = sin * scale
    steps = QUART // SEED
    times = lax.broadcasted_iota(jnp.int32, (steps, NF), 0) * SEED
    cos, sin = cos_sin(times * bins)
    first[0] = cos
    first[1] = sin
    for q in range(N_Y):
        turn = (bins * q) & 3
        rot[q:q + 1, :] = jnp.where(turn == 0, 1.0, jnp.where(turn == 2, -1.0, 0.0))
        rot[4 + q:5 + q, :] = jnp.where(turn == 1, 1.0, jnp.where(turn == 3, -1.0, 0.0))

    def make_rows(i, carry):
        c0 = first[0, pl.ds(i, 1), :]
        s0 = first[1, pl.ds(i, 1), :]
        at = pl.ds(pl.multiple_of(i * SEED, SEED), SEED)
        c1 = seed[0]
        s1 = seed[1]
        tab[at, :NF] = (c0 * c1 - s0 * s1).astype(jnp.bfloat16)
        tab[at, NF:] = (-(s0 * c1 + c0 * s1)).astype(jnp.bfloat16)
        return carry

    lax.fori_loop(0, steps, make_rows, 0)

    r_dev = live_ref.shape[1]
    lane = lax.broadcasted_iota(jnp.int32, (r_sub, r_dev), 1)
    line = lax.broadcasted_iota(jnp.int32, (r_sub, r_dev), 0) + me * r_sub
    weights = []
    for s in range(shots):
        flags = jnp.where(lane == line, live_ref[s:s + 1, :].astype(jnp.float32), 0.0)
        weights.append(jnp.sum(flags, axis=1, keepdims=True))

    def loop(n, body):
        if UNROLL:
            for i in range(n):
                body(i, 0)
        else:
            lax.fori_loop(0, n, body, 0)

    def forward_group(s, low, high):
        weight = weights[s]
        width = 256
        for g in range(low, high):
            wait_bytes(xbuf.at[s, g * rows:(g + 1) * rows], in_recv.at[s, g])

        def tile(n, carry):
            lanes = pl.ds(pl.multiple_of(n * width, width), width)
            lanes_im = pl.ds(pl.multiple_of(NF + n * width, width), width)
            traces = xbuf[s, low * rows:high * rows]
            re = jnp.dot(traces, tab[:, lanes], preferred_element_type=jnp.float32)
            im = jnp.dot(traces, tab[:, lanes_im], preferred_element_type=jnp.float32)
            x_re = None if low == 0 else acc[0, :, lanes]
            x_im = None if low == 0 else acc[1, :, lanes]
            for g in range(low, high):
                q = (y - ORDER[g] + N_Y) % N_Y
                c = rot[pl.ds(q, 1), lanes]
                d = rot[pl.ds(4 + q, 1), lanes]
                here = slice((g - low) * rows, (g - low + 1) * rows)
                a_re = c * re[here] + d * im[here]
                a_im = c * im[here] - d * re[here]
                x_re = a_re if x_re is None else x_re + a_re
                x_im = a_im if x_im is None else x_im + a_im
            if high < N_Y:
                acc[0, :, lanes] = x_re
                acc[1, :, lanes] = x_im
                return carry
            obs_re = weight * x_re[:r_sub]
            obs_im = weight * x_im[:r_sub]
            syn_re = weight * x_re[r_sub:]
            syn_im = weight * x_im[r_sub:]
            spec[s, 0, :, lanes] = obs_re
            spec[s, 1, :, lanes] = obs_im
            spec[s, 2, :, lanes] = syn_re
            spec[s, 3, :, lanes] = syn_im
            sums = (
                jnp.sum(syn_re * obs_re + syn_im * obs_im, axis=0, keepdims=True),
                jnp.sum(syn_re * obs_im - syn_im * obs_re, axis=0, keepdims=True),
                jnp.sum(syn_re * syn_re + syn_im * syn_im, axis=0, keepdims=True),
            )
            for q in range(3):
                for h in range(width // 128):
                    part[s, pl.ds(q * 8 + n * (width // 128) + h, 1), :] = sums[q][:, h * 128:(h + 1) * 128]
            return carry

        loop(NF // width, tile)

    def forward(s):
        for low, high in GROUPS:
            forward_group(s, low, high)

    def reduce_start(s, k):
        src, buf, _, size, pos, send, recv = stage(k)
        for peer in reduce_peers(k):
            pltpu.make_async_remote_copy(
                src_ref=src.at[s], dst_ref=buf.at[s, pos], send_sem=send.at[s], recv_sem=recv.at[s],
                device_id=peer, device_id_type=MESH).start()
        buf[s, pl.ds(pos, 1)] = src[s][None]

    def reduce_finish(s, k):
        _, buf, dst, size, _, _, recv = stage(k)
        if size > 1:
            wait_bytes(buf.at[s, pl.ds(0, size - 1)], recv.at[s])
        dst[s] = jnp.sum(buf[s], axis=0)

    def inverse(s):
        cross_re = total[s, 0:8, :]
        cross_im = total[s, 8:16, :]
        power = total[s, 16:24, :]
        denom = power + 0.001 * jnp.max(power)
        wrow[0:8, :] = cross_re / denom
        wrow[8:16, :] = cross_im / denom

        def block(k, carry):
            lanes = pl.ds(pl.multiple_of(k * 128, 128), 128)
            lanes_im = pl.ds(pl.multiple_of(NF + k * 128, 128), 128)
            w_re = wrow[pl.ds(k, 1), :]
            w_im = wrow[pl.ds(8 + k, 1), :]
            obs_re, obs_im, syn_re, syn_im = (spec[s, i, :, lanes] for i in range(4))
            re = w_re * syn_re - w_im * syn_im - obs_re
            im = w_re * syn_im + w_im * syn_re - obs_im
            for q in range(N_Y):
                c = rot[q:q + 1, lanes]
                d = rot[4 + q:5 + q, lanes]
                here = slice(q * r_sub, (q + 1) * r_sub)
                res[here, lanes] = (c * re - d * im).astype(jnp.bfloat16)
                res[here, lanes_im] = (d * re + c * im).astype(jnp.bfloat16)
            return carry

        loop(NF // 128, block)

        for dj in TILES:
            _, pj = peer_of(y, j, 0, dj)
            cols = pl.ds(pl.multiple_of(pj * SPAN, SPAN), SPAN)
            sums = lax.dot_general(res[...], tab[cols, :], (((1,), (1,)), ((), ())),
                                   preferred_element_type=jnp.float32)
            outbuf[s, :, cols] = (2.0 * sums).astype(jnp.bfloat16)
            for dy in (2, 3, 1, 0):
                py, _ = peer_of(y, j, dy, 0)
                src = outbuf.at[s, pl.ds(pl.multiple_of(py * r_sub, r_sub), r_sub), cols]
                dst = out_ref.at[s, pl.ds(pl.multiple_of(me * r_sub, r_sub), r_sub), :]
                if dy == 0 and dj == 0:
                    pltpu.make_async_copy(src, dst, out_recv.at[s]).start()
                else:
                    pltpu.make_async_remote_copy(
                        src_ref=src, dst_ref=dst, send_sem=out_send.at[s], recv_sem=out_recv.at[s],
                        device_id={"tf": py * N_J + pj}, device_id_type=MESH).start()

    forward(0)
    reduce_start(0, 0)
    send_in(1, SLOTS[BATCH[0]:BATCH[1]])
    reduce_finish(0, 0)
    reduce_start(0, 1)
    send_in(1, SLOTS[BATCH[1]:])
    reduce_finish(0, 1)
    reduce_start(0, 2)
    forward(1)
    reduce_start(1, 0)
    reduce_finish(0, 2)
    inverse(0)
    reduce_finish(1, 0)
    reduce_start(1, 1)
    reduce_finish(1, 1)
    reduce_start(1, 2)
    reduce_finish(1, 2)
    inverse(1)

    for s in range(shots):
        wait_bytes(out_ref.at[s], out_recv.at[s])
    for s in range(shots):
        sent = obs_ref.at[s, pl.ds(0, (N_TF - 1) * r_sub), :]
        wait_bytes(sent, in_send.at[s])
        wait_bytes(sent, in_send.at[s])
        wait_bytes(out_ref.at[s, pl.ds(0, (N_TF - 1) * r_sub), :], out_send.at[s])
        wait_bytes(from_a.at[s, pl.ds(0, 2 * N_Y - 1)], a_send.at[s])
        if n_x > 1:
            wait_bytes(from_x.at[s, pl.ds(0, n_x - 1)], x_send.at[s])
        wait_bytes(from_z.at[s, pl.ds(0, n_z - 1)], z_send.at[s])


def on_device(n_rcv, observed, synthetic, live, bins):
    shots, r_dev, _ = observed.shape
    r_sub = r_dev // N_TF
    n_x = min(4, n_rcv)
    n_zh = n_rcv // n_x

    def body(*refs):
        kernel(r_sub, n_x, n_zh, *refs)

    f32, bf16 = jnp.float32, jnp.bfloat16
    sums = (24, 128)
    dma = pltpu.SemaphoreType.DMA
    return pl.pallas_call(
        body,
        out_shape=jax.ShapeDtypeStruct(observed.shape, bf16),
        in_specs=[pl.BlockSpec(memory_space=pl.ANY)] * 4,
        out_specs=pl.BlockSpec(memory_space=pl.ANY),
        scratch_shapes=[
            pltpu.VMEM((1, NF), jnp.int32),
            pltpu.VMEM(live.shape, jnp.int32),
            pltpu.VMEM((shots, N_Y * 2 * r_sub, QUART), bf16),
            pltpu.VMEM((QUART, 2 * NF), bf16),
            pltpu.VMEM((2, SEED, NF), f32),
            pltpu.VMEM((2, QUART // SEED, NF), f32),
            pltpu.VMEM((8, NF), f32),
            pltpu.VMEM((shots, 4, r_sub, NF), f32),
            pltpu.VMEM((N_Y * r_sub, 2 * NF), bf16),
            pltpu.VMEM((shots, N_Y * r_sub, QUART), bf16),
            pltpu.VMEM((16, 128), f32),
            pltpu.VMEM((2, 2 * r_sub, NF), f32),
            pltpu.VMEM((shots,) + sums, f32),
            pltpu.VMEM((shots, 2 * N_Y) + sums, f32),
            pltpu.VMEM((shots,) + sums, f32),
            pltpu.VMEM((shots, n_x) + sums, f32),
            pltpu.VMEM((shots,) + sums, f32),
            pltpu.VMEM((shots, 2 * n_zh) + sums, f32),
            pltpu.VMEM((shots,) + sums, f32),
        ] + [dma((shots,))] * 2 + [dma((shots, N_Y))] + [dma((shots,))] * 8,
        compiler_params=pltpu.CompilerParams(
            collective_id=0, has_side_effects=True, vmem_limit_bytes=60 * 2 ** 20),
    )(bins.reshape(1, NF), live, observed, synthetic)


def solution(mesh):
    n_rcv = mesh.shape["rcv"]

    def run(*args):
        return on_device(n_rcv, *args)

    in_specs = (P(None, "rcv", "tf"), P(None, "rcv", "tf"), P(None, "rcv"), P())
    out_specs = P(None, "rcv", "tf")
    return jax.shard_map(run, mesh=mesh, in_specs=in_specs, out_specs=out_specs, check_vma=False)
```
